128 devices in a mesh: dp: 8 (over x, y_lo), seq: 16 (over z, y_hi, core).
Axes of the slice: x: 4, y: 4 (y_hi: 2, y_lo: 2; y = y_hi * 2 + y_lo), z: 4, core: 2. Of those that a mesh axis runs over, the one named last changes fastest.
Arguments:
- queries: bfloat16 [8, 3072, 4096], P('dp', 'seq'), may hold values from -9 to 9
- key_rows: bfloat16 [8, 3072, 4096], P('dp', 'seq'), may hold values from -9 to 9
- value_rows: bfloat16 [8, 3072, 4096], P('dp', 'seq'), may hold values from -12 to 12
- residual: bfloat16 [8, 3072, 5120], P('dp', 'seq'), may hold values from -6 to 6
- gate_scale: float32 [8, 5120], P('dp'), may hold values from 0.25 to 1.5
- out_weight: bfloat16 [4096, 5120], P('seq'), may hold values from -0.09375 to 0.09375
- adapter_down: bfloat16 [4096, 64], replicated, may hold values from -0.09375 to 0.09375
- adapter_up: bfloat16 [64, 5120], replicated, may hold values from -0.75 to 0.75
- cotangent: bfloat16 [8, 3072, 5120], P('dp', 'seq'), may hold values from -0.038085938 to 0.038085938
- clip_lengths: int32 [8], P('dp'), may hold values from 1536 to 3072, as said below
Outputs:
- block_out: bfloat16 [8, 3072, 5120], P('dp', 'seq')
- grad_down: float32 [4096, 64], replicated
- grad_up: float32 [64, 5120], replicated
The draws below stay inside these ranges and needn't reach their ends.
Inputs may be any that keep to these rules, and one draw needn't show every extreme that they name: `clip_lengths`: some clip has all 3072 tokens valid.
All inputs are finite; a program needn't handle non-finite values.
Results may differ from the reference program's by a relative error of at most 0.012.
Values may be sent and summed in bfloat16 or wider, within the bound.
A program may use at most 192 MiB of HBM per device.

```python
import jax
import jax.numpy as jnp
from jax import lax

D = 5120
HEADS = 32
HEAD_DIM = 128
RANK = 64
SEQLEN = 3072
CLIPS = 8
HD = 4096
OUT_GROUPS = 16


def draw_queries(key, part):
    key = jax.random.fold_in(key, 11)
    shape_all = (CLIPS, SEQLEN, HEADS, HEAD_DIM)
    values = jnp.clip(1.5 * jax.random.normal(key, shape_all, jnp.float32), -9.0, 9.0)
    return values.reshape(CLIPS, SEQLEN, HEADS * HEAD_DIM).astype(jnp.bfloat16)


def draw_key_rows(key, part):
    key = jax.random.fold_in(key, 13)
    shape_all = (CLIPS, SEQLEN, HEADS, HEAD_DIM)
    values = jnp.clip(1.5 * jax.random.normal(key, shape_all, jnp.float32), -9.0, 9.0)
    return values.reshape(CLIPS, SEQLEN, HEADS * HEAD_DIM).astype(jnp.bfloat16)


def draw_clip_lengths(key, part):
    key = jax.random.fold_in(key, 17)
    first_key, second_key = jax.random.split(key)
    drawn = jax.random.randint(first_key, (CLIPS,), SEQLEN // 2, SEQLEN + 1, dtype=jnp.int32)
    chosen = jax.random.randint(second_key, (), 0, CLIPS, dtype=jnp.int32)
    return jnp.where(jnp.arange(CLIPS, dtype=jnp.int32) == chosen, SEQLEN, drawn).astype(jnp.int32)


def block_levels(rng, dims, shards, least, high):
    loudness = 1.0
    for dim, parts in shards:
        draws = jax.random.uniform(jax.random.fold_in(jax.random.fold_in(rng, 6), dim), (parts,), jnp.float32, least / len(shards), high / len(shards))
        loudness = loudness * jnp.repeat(jnp.exp(draws), dims[dim] // parts).reshape((-1,) + (1,) * (len(dims) - 1 - dim))
    return loudness


def gaussian(rng, dims, width, limit, cuts=(), held_as=jnp.bfloat16):
    gain = block_levels(rng, dims, cuts, -0.22, 0.18) if cuts else 1.0
    values = jax.random.normal(rng, dims, jnp.float32) * width * gain
    return jnp.minimum(jnp.maximum(values, -limit), limit).astype(held_as)


def setup_inputs(seed: int = 0) -> dict:
    keys = jax.random.split(jax.random.key(seed), 11)
    return {
        "queries": draw_queries(jax.random.fold_in(keys[10], 71), 0),
        "key_rows": draw_key_rows(jax.random.fold_in(keys[10], 71), 0),
        "value_rows": gaussian(keys[2], (CLIPS, SEQLEN, HD), 2.0, 12.0, ((0, 8), (1, 16))),
        "residual": gaussian(keys[3], (CLIPS, SEQLEN, D), 1.0, 6.0, ((0, 8), (1, 16))),
        "gate_scale": jnp.clip(0.25 + 1.25 * jax.random.uniform(keys[4], (CLIPS, D), jnp.float32) ** block_levels(keys[4], (CLIPS, D), ((0, 8),), -0.2, 0.2), 0.25, 1.5),
        "out_weight": gaussian(keys[5], (HD, D), HD ** -0.5, 0.09375, ((0, 16),)),
        "adapter_down": gaussian(keys[6], (HD, RANK), HD ** -0.5, 0.09375),
        "adapter_up": gaussian(keys[7], (RANK, D), RANK ** -0.5, 0.75),
        "cotangent": gaussian(keys[8], (CLIPS, SEQLEN, D), (1.0 / (SEQLEN * CLIPS) ** 0.5), 0.038085938, ((0, 8), (1, 16))),
        "clip_lengths": draw_clip_lengths(jax.random.fold_in(keys[10], 71), 0),
    }


def attend_head(query_head, key_head, value_head, live_keys):
    factor = HEAD_DIM ** -0.5
    scores = jnp.dot(query_head, key_head.T, preferred_element_type=jnp.float32) * factor
    scores = jnp.where(live_keys[None, :], scores, -1e30)
    largest = jnp.max(scores, axis=1, keepdims=True)
    powers = jnp.exp(scores - largest)
    weights = (powers / jnp.sum(powers, axis=1, keepdims=True)).astype(jnp.bfloat16)
    return jnp.dot(weights, value_head, preferred_element_type=jnp.float32).astype(jnp.bfloat16)


def column_slice(matrix_in, first_col):
    return lax.dynamic_slice_in_dim(matrix_in, first_col, HEAD_DIM, 1)


def attend_bundle(bundle):
    query_clip, key_clip, value_clip, length = bundle
    live_keys = jnp.arange(SEQLEN, dtype=jnp.int32) < length

    def per_head(head_index):
        first_col = (head_index * HEAD_DIM).astype(jnp.int32)
        return attend_head(column_slice(query_clip, first_col), column_slice(key_clip, first_col),
                           column_slice(value_clip, first_col), live_keys)

    outputs = lax.map(per_head, jnp.arange(HEADS, dtype=jnp.int32))
    return outputs.transpose(1, 0, 2).reshape(SEQLEN, HEADS * HEAD_DIM)


def reference(queries, key_rows, value_rows, residual, gate_scale, out_weight, adapter_down, adapter_up, cotangent, clip_lengths):
    attended = lax.map(attend_bundle, (queries, key_rows, value_rows, clip_lengths))
    row_count = CLIPS * SEQLEN
    flat_rows = attended.reshape(row_count, HD)
    group_cols = HD // OUT_GROUPS
    pieces = flat_rows.reshape(row_count, OUT_GROUPS, group_cols).transpose(1, 0, 2)
    weight_groups = out_weight.reshape(OUT_GROUPS, group_cols, D)

    def add_group(running, operands):
        product = jnp.dot(operands[0], operands[1], preferred_element_type=jnp.float32)
        rounded = lax.optimization_barrier(product.astype(jnp.bfloat16)).astype(jnp.float32)
        return running + rounded, 0

    base, _ = lax.scan(add_group, jnp.zeros((row_count, D), jnp.float32), (pieces, weight_groups))
    low_rank = jnp.dot(flat_rows, adapter_down, preferred_element_type=jnp.float32).astype(jnp.bfloat16)
    delta = jnp.dot(low_rank, adapter_up, preferred_element_type=jnp.float32)
    gate_rows = jnp.repeat(gate_scale, SEQLEN, axis=0)
    block_out = (residual.reshape(row_count, D).astype(jnp.float32) + gate_rows * (base + delta)).astype(jnp.bfloat16)
    scaled = (cotangent.reshape(row_count, D).astype(jnp.float32) * gate_rows).astype(jnp.bfloat16)
    grad_up = jnp.dot(low_rank.T, scaled, preferred_element_type=jnp.float32)
    low_grad = jnp.dot(scaled, adapter_up.T, preferred_element_type=jnp.float32).astype(jnp.bfloat16)
    grad_down = jnp.dot(flat_rows.T, low_grad, preferred_element_type=jnp.float32)
    return block_out.reshape(CLIPS, SEQLEN, D), grad_down, grad_up
```

```python
import jax
import jax.numpy as jnp
import numpy as np
from jax import lax
from jax.experimental import pallas as pl
from jax.experimental.pallas import tpu as pltpu
from jax.sharding import Mesh
from jax.sharding import PartitionSpec as P

AXES = ("x", "yl", "z", "yh", "c")
DP = ("x", "yl")
SEQ = ("z", "yh", "c")
MESH = pl.DeviceIdType.MESH
HEAD = 128
RANK = 64
TOK = 192
CHIP = 2 * TOK
SEQLEN = 3072
D = 5120
QUARTER = D // 4
BQ = 768
KC = 512
SCALE = float(HEAD**-0.5 * np.log2(np.e))
F32 = jnp.float32
BF16 = jnp.bfloat16


def kernel(
    len_ref, q, k, v, res, gate, w, down, up, cot,
    out, gd, gu,
    qkv, bias, att, ag, wq, lg, dn, low, ps, pk, pr, yb,
    gdp, gup, l0, l1, g0, gs, g1, g2u, g2d, gda,
    snd, qkv_sem, lg_sem, ag_sem, wq_sem, fwd_sem, lr_sem, g0_sem, g1_sem, g2u_sem, g2d_sem, g3_sem, g4_sem, pr_sem, yb_sem,
):
    x, yl, z, yh, c = (lax.axis_index(a) for a in AXES)
    s = z * 4 + yh * 2 + c
    j = z * 2 + yh
    dp = x * 2 + yl
    own = pl.ds(s * TOK, TOK)

    def seq_peer(p):
        return {"z": p // 4, "yh": lax.rem(p, 4) // 2, "c": lax.rem(p, 2)}

    def chip_peer(p):
        return {"z": p // 2, "yh": lax.rem(p, 2)}

    def dp_peer(p):
        return {"x": p // 2, "yl": lax.rem(p, 2)}

    other = {"c": 1 - c}

    def remote(src, dst, sem, dev):
        return pltpu.make_async_remote_copy(
            src_ref=src, dst_ref=dst, send_sem=snd, recv_sem=sem, device_id=dev, device_id_type=MESH
        )

    def landed(ref, sem):
        pltpu.make_async_copy(ref, ref, sem).wait()

    barrier = pltpu.get_barrier_semaphore()

    def greet_seq(d, _):
        pl.semaphore_signal(barrier, inc=1, device_id=seq_peer(lax.rem(s + d, 16)), device_id_type=MESH)
        return 0

    def greet_dp(d, _):
        pl.semaphore_signal(barrier, inc=1, device_id=dp_peer(lax.rem(dp + d, 8)), device_id_type=MESH)
        return 0

    lax.fori_loop(1, 16, greet_seq, 0)
    lax.fori_loop(1, 8, greet_dp, 0)
    pl.semaphore_wait(barrier, 22)

    def send_head(h):
        def columns(p):
            return pl.ds(pl.multiple_of(p * 256 + h * HEAD, HEAD), HEAD)

        for a, src in enumerate((q, k, v)):
            pltpu.make_async_copy(src.at[:, columns(s)], qkv.at[h, a, own], qkv_sem.at[h]).start()

        def step(d, _):
            p = lax.rem(s + d, 16)
            for a, src in enumerate((q, k, v)):
                remote(src.at[:, columns(p)], qkv.at[h, a, own], qkv_sem.at[h], seq_peer(p)).start()
            return 0

        lax.fori_loop(1, 16, step, 0)

    send_head(0)

    bias[...] = jnp.where(lax.broadcasted_iota(jnp.int32, (SEQLEN, HEAD), 0) < len_ref[0], 0.0, -1e30)
    def scaled(cols):
        return (cot[:, cols].astype(F32) * gate[:, cols]).astype(BF16)

    low_grad = jnp.zeros((TOK, RANK), F32)
    for t in range(5):
        cols = slice(t * 1024, (t + 1) * 1024)
        low_grad += lax.dot_general(scaled(cols), up[:, cols], (((1,), (1,)), ((), ())), preferred_element_type=F32)
    lg[own, :] = jnp.zeros((TOK, HEAD), BF16)
    lg[own, 0:RANK] = low_grad.astype(BF16)

    def send_low_grad(d, _):
        remote(lg.at[own], lg.at[own], lg_sem, seq_peer(lax.rem(s + d, 16))).start()
        return 0

    lax.fori_loop(1, 16, send_low_grad, 0)

    for h in range(2):
        for t in range(8):
            dn[h, t * HEAD : (t + 1) * HEAD, :] = down[pl.ds(512 * t + 256 * c + 128 * h, HEAD), :]

    def attend(h):
        def chunk(i, total):
            zz = lax.rem(z + 1 + i, 4)
            rows = pl.ds(pl.multiple_of(zz * BQ, BQ), BQ)
            queries = qkv[h, 0, rows, :]
            scores, top = [], None
            for t in range(SEQLEN // KC):
                keys = slice(t * KC, (t + 1) * KC)
                part = lax.dot_general(qkv[h, 1, keys, :], queries, (((1,), (1,)), ((), ())), preferred_element_type=F32)
                part = part + jnp.concatenate([bias[keys, :]] * (BQ // HEAD), 1)
                scores.append(part)
                largest = jnp.max(part, axis=0, keepdims=True)
                top = largest if top is None else jnp.maximum(top, largest)
            top = top * SCALE
            mixed, weight = None, None
            for t in range(SEQLEN // KC):
                keys = slice(t * KC, (t + 1) * KC)
                powers = jnp.exp2(scores[t] * SCALE - top)
                summed = jnp.sum(powers, axis=0, keepdims=True)
                product = lax.dot_general(
                    qkv[h, 2, keys, :], powers.astype(BF16), (((0,), (0,)), ((), ())), preferred_element_type=F32
                )
                mixed = product if mixed is None else mixed + product
                weight = summed if weight is None else weight + summed
            mixed = mixed / weight
            att[h, rows, :] = mixed.T.astype(BF16)

            def piece(yy):
                src = att.at[h, pl.ds(pl.multiple_of(zz * BQ + yy * CHIP, CHIP), CHIP), :]
                return src, ag.at[h, x, :, pl.ds(pl.multiple_of(j * HEAD, HEAD), HEAD)]

            src, dst = piece(1 - yh)
            remote(src, dst, ag_sem.at[h], chip_peer(zz * 2 + 1 - yh)).start()
            src, dst = piece(yh)

            @pl.when(i < 3)
            def _():
                remote(src, dst, ag_sem.at[h], chip_peer(zz * 2 + yh)).start()

            @pl.when(i == 3)
            def _():
                pltpu.make_async_copy(src, dst, ag_sem.at[h]).start()

            return total + jnp.dot(mixed.astype(BF16), lg[rows, :], preferred_element_type=F32)

        gdp[h * HEAD : (h + 1) * HEAD, :] = lax.fori_loop(0, SEQLEN // BQ, chunk, jnp.zeros((HEAD, HEAD), F32))

    landed(qkv.at[0], qkv_sem.at[0])
    send_head(1)
    landed(lg.at[pl.ds(0, 15 * TOK)], lg_sem)
    attend(0)
    landed(qkv.at[1], qkv_sem.at[1])

    def weight_piece(h):
        src = w.at[pl.ds(h * HEAD, HEAD), pl.ds(pl.multiple_of(x * QUARTER, QUARTER), QUARTER)]
        return src, wq.at[h, pl.ds(pl.multiple_of(j * HEAD, HEAD), HEAD), :]

    for h in range(2):
        src, dst = weight_piece(h)
        pltpu.make_async_copy(src, dst, wq_sem).start()

        def send_weight(d, _):
            remote(src, dst, wq_sem, chip_peer(lax.rem(j + d, 8))).start()
            return 0

        lax.fori_loop(1, 8, send_weight, 0)

    def forward(h):
        landed(ag.at[h, x], ag_sem.at[h])

        def step(d, _):
            remote(ag.at[h, x], ag.at[h, x], fwd_sem.at[h, x], {"x": lax.rem(x + d, 4)}).start()
            return 0

        lax.fori_loop(1, 4, step, 0)

    forward(0)
    attend(1)
    forward(1)

    l0[...] = jnp.zeros((CHIP, HEAD), F32)
    l0[:, 0:RANK] = jnp.dot(ag[0, x], dn[0], preferred_element_type=F32) + jnp.dot(ag[1, x], dn[1], preferred_element_type=F32)
    remote(l0.at[pl.ds((1 - c) * TOK, TOK)], l1, lr_sem, other).start()
    landed(l1, lr_sem)
    low[...] = (l0[pl.ds(c * TOK, TOK), 0:RANK] + l1[:, 0:RANK]).astype(BF16)

    for t in range(5):
        cols = slice(t * 1024, (t + 1) * 1024)
        gup[:, cols] = lax.dot_general(low[...], scaled(cols), (((0,), (0,)), ((), ())), preferred_element_type=F32)
    remote(gup.at[pl.ds((1 - c) * 32, 32)], g0, g0_sem, other).start()
    landed(g0, g0_sem)
    gs[...] = gup[pl.ds(c * 32, 32), :] + g0[...]

    def columns640(p):
        return pl.ds(pl.multiple_of(p * 640, 640), 640)

    def reduce_up(d, _):
        p = lax.rem(j + d, 8)
        remote(gs.at[:, columns640(p)], g1.at[j], g1_sem, chip_peer(p)).start()
        return 0

    lax.fori_loop(1, 8, reduce_up, 0)
    pltpu.make_async_copy(gs.at[:, columns640(j)], g1.at[j], g1_sem).start()
    landed(g1, g1_sem)
    total = g1[0]
    for t in range(1, 8):
        total = total + g1[t]
    g2u[dp] = total
    g2d[dp] = gdp[...]

    def over_clips(d, _):
        dev = dp_peer(lax.rem(dp + d, 8))
        remote(g2u.at[dp], g2u.at[dp], g2u_sem, dev).start()
        remote(g2d.at[dp], g2d.at[dp], g2d_sem, dev).start()
        return 0

    lax.fori_loop(1, 8, over_clips, 0)
    landed(g2u.at[pl.ds(0, 7)], g2u_sem)
    landed(g2d.at[pl.ds(0, 7)], g2d_sem)
    total = g2u[0]
    total_down = g2d[0]
    for t in range(1, 8):
        total = total + g2u[t]
        total_down = total_down + g2d[t]
    g0[:, 0:640] = total
    rank_rows = pl.ds(pl.multiple_of(c * 32, 32), 32)
    up_piece = gu.at[rank_rows, columns640(j)]
    gda[c, j] = total_down
    pltpu.make_async_copy(g0.at[:, 0:640], up_piece, g3_sem.at[0]).start()

    def spread(d, _):
        dev = chip_peer(lax.rem(j + d, 8))
        remote(g0.at[:, 0:640], up_piece, g3_sem.at[0], dev).start()
        remote(gda.at[c, j], gda.at[c, j], g4_sem.at[0], dev).start()
        return 0

    lax.fori_loop(1, 8, spread, 0)

    landed(wq, wq_sem)
    for d in range(4):
        xx = lax.rem(x + 4 - d, 4)
        if d:
            for h in range(2):
                landed(ag.at[h, xx], fwd_sem.at[h, xx])

        def block(t, _):
            cols = pl.ds(pl.multiple_of(t * 256, 256), 256)
            part = jnp.dot(ag[0, xx], wq[0, :, cols], preferred_element_type=F32)
            part += jnp.dot(ag[1, xx], wq[1, :, cols], preferred_element_type=F32)
            first, second = part[:TOK], part[TOK:]
            pk[d, :, cols] = jnp.where(c == 0, first, second).astype(BF16)
            ps[d, :, cols] = jnp.where(c == 0, second, first).astype(BF16)
            return 0

        lax.fori_loop(0, QUARTER // 256, block, 0)
        remote(ps.at[d], pr.at[d], pr_sem.at[d], other).start()

    for d in range(4):
        landed(pr.at[d], pr_sem.at[d])
        pk[d] = (pk[d].astype(F32) + pr[d].astype(F32)).astype(BF16)
        if d:
            remote(pk.at[d], yb.at[x], yb_sem.at[x], {"x": lax.rem(x + 4 - d, 4)}).start()

    landed(gu.at[pl.ds(0, 32)], g3_sem.at[0])
    landed(gda.at[0, pl.ds(0, 7)], g4_sem.at[0])
    remote(gu.at[rank_rows], gu.at[rank_rows], g3_sem.at[1], other).start()
    remote(gda.at[c], gda.at[c], g4_sem.at[1], other).start()

    for d in range(4):
        xx = lax.rem(x + d, 4)
        if d:
            landed(yb.at[xx], yb_sem.at[xx])
        cols = pl.ds(pl.multiple_of(xx * QUARTER, QUARTER), QUARTER)
        base = (yb[xx] if d else pk[0]).astype(F32)
        delta = jnp.dot(low[...], up[:, cols], preferred_element_type=F32)
        out[:, cols] = (res[:, cols].astype(F32) + gate[:, cols] * (base + delta)).astype(BF16)

    landed(gu.at[pl.ds(0, 32)], g3_sem.at[1])
    landed(gda.at[0], g4_sem.at[1])
    for cc in range(2):
        for t in range(8):
            gd[(2 * t + cc) * 256 : (2 * t + cc + 1) * 256, :] = gda[cc, t, :, 0:RANK]

    def drain(count, ref):
        def step(_, carry):
            landed(ref, snd)
            return carry

        lax.fori_loop(0, count, step, 0)

    drain(90, qkv.at[0, 0, pl.ds(0, TOK)])
    drain(15, lg.at[pl.ds(0, TOK)])
    drain(14, att.at[0, pl.ds(0, CHIP), :])
    drain(14, wq.at[0, pl.ds(0, HEAD), :])
    drain(6, ag.at[0, 0])
    drain(1, l1)
    drain(1, g0)
    drain(7, g1.at[0])
    drain(7, g2u.at[0])
    drain(7, g2d.at[0])
    drain(7, g1.at[0])
    drain(7, gda.at[0, 0])
    drain(4, ps.at[0])
    drain(3, pk.at[0])
    drain(1, gu.at[pl.ds(0, 32)])
    drain(1, gda.at[0])


def on_device(q, k, v, res, gate, w, down, up, cot, lengths):
    vmem = pl.BlockSpec(memory_space=pltpu.VMEM)
    hbm = pl.BlockSpec(memory_space=pl.ANY)
    dma = pltpu.SemaphoreType.DMA
    out, gd, gu = pl.pallas_call(
        kernel,
        out_shape=(
            jax.ShapeDtypeStruct((TOK, D), BF16),
            jax.ShapeDtypeStruct((4096, RANK), F32),
            jax.ShapeDtypeStruct((RANK, D), F32),
        ),
        in_specs=[pl.BlockSpec(memory_space=pltpu.SMEM), hbm, hbm, hbm, vmem, vmem, hbm, vmem, vmem, vmem],
        out_specs=(vmem, vmem, vmem),
        scratch_shapes=[
            pltpu.VMEM((2, 3, SEQLEN, HEAD), BF16),
            pltpu.VMEM((SEQLEN, HEAD), F32),
            pltpu.VMEM((2, SEQLEN, HEAD), BF16),
            pltpu.VMEM((2, 4, CHIP, 1024), BF16),
            pltpu.VMEM((2, 1024, QUARTER), BF16),
            pltpu.VMEM((SEQLEN, HEAD), BF16),
            pltpu.VMEM((2, 1024, RANK), BF16),
            pltpu.VMEM((TOK, RANK), BF16),
            pltpu.VMEM((4, TOK, QUARTER), BF16),
            pltpu.VMEM((4, TOK, QUARTER), BF16),
            pltpu.VMEM((4, TOK, QUARTER), BF16),
            pltpu.VMEM((4, TOK, QUARTER), BF16),
            pltpu.VMEM((256, HEAD), F32),
            pltpu.VMEM((RANK, D), F32),
            pltpu.VMEM((CHIP, HEAD), F32),
            pltpu.VMEM((TOK, HEAD), F32),
            pltpu.VMEM((32, D), F32),
            pltpu.VMEM((32, D), F32),
            pltpu.VMEM((8, 32, 640), F32),
            pltpu.VMEM((8, 32, 640), F32),
            pltpu.VMEM((8, 256, HEAD), F32),
            pltpu.VMEM((2, 8, 256, HEAD), F32),
            dma,
            dma((2,)),
            dma,
            dma((2,)),
            dma,
            dma((2, 4)),
            dma,
            dma,
            dma,
            dma,
            dma,
            dma((2,)),
            dma((2,)),
            dma((4,)),
            dma((4,)),
        ],
        compiler_params=pltpu.CompilerParams(collective_id=1, has_side_effects=True, vmem_limit_bytes=63 * 2**20),
        cost_estimate=pl.CostEstimate(flops=18 * 10**9, bytes_accessed=30 * 10**6, transcendentals=19 * 10**6),
    )(lengths, q[0], k[0], v[0], res[0], gate, w, down, up, cot[0])
    return out[None], gd, gu


def solution(mesh):
    inner = Mesh(mesh.devices.reshape(4, 2, 4, 2, 2), AXES)
    return jax.shard_map(
        on_device,
        mesh=inner,
        in_specs=(
            P(DP, SEQ, None),
            P(DP, SEQ, None),
            P(DP, SEQ, None),
            P(DP, SEQ, None),
            P(DP, None),
            P(SEQ, None),
            P(),
            P(),
            P(DP, SEQ, None),
            P(DP),
        ),
        out_specs=(P(DP, SEQ, None), P(), P()),
        check_vma=False,
    )
```

```python
import jax
import jax.numpy as jnp
import numpy as np
from jax import lax
from jax.experimental import pallas as pl
from jax.experimental.pallas import tpu as pltpu
from jax.sharding import Mesh
from jax.sharding import PartitionSpec as P

AXES = ("x", "yl", "z", "yh", "c")
DP = ("x", "yl")
SEQ = ("z", "yh", "c")
MESH = pl.DeviceIdType.MESH
HEAD = 128
RANK = 64
TOK = 192
CHIP = 2 * TOK
SEQLEN = 3072
D = 5120
QUARTER = D // 4
BQ = 768
KC = 512
SCALE = float(HEAD**-0.5 * np.log2(np.e))
F32 = jnp.float32
BF16 = jnp.bfloat16


def kernel(
    len_ref, q, k, v, res_hbm, gate, w, down, up_hbm, cot_hbm,
    out, gd, gu,
    qkv, bias, att, ag, wq, lgc, dn, low, ps, pk, pr, yb,
    res, up, cot, gup, l0, l1, g0, gs, g1, gdq, g1d, g2u, g2d, g3u, gda,
    snd, load_sem, qkv_sem, lg_sem, ag_sem, wq_sem, wl_sem, f1_sem, f2_sem, lr_sem, g0_sem, g1_sem, g1d_sem, g2u_sem, g2d_sem,
    g3u_sem, g3d_sem, g4_sem, pr_sem, yb_sem,
):
    x, yl, z, yh, c = (lax.axis_index(a) for a in AXES)
    s = z * 4 + yh * 2 + c
    j = z * 2 + yh
    dp = x * 2 + yl
    right, left = lax.rem(x + 1, 4), lax.rem(x + 3, 4)
    own = pl.ds(s * TOK, TOK)
    pending = []

    def seq_peer(p):
        return {"z": p // 4, "yh": lax.rem(p, 4) // 2, "c": lax.rem(p, 2)}

    def chip_peer(p):
        return {"z": p // 2, "yh": lax.rem(p, 2)}

    def dp_peer(p):
        return {"x": p // 2, "yl": lax.rem(p, 2)}

    other = {"c": 1 - c}

    def remote(src, dst, sem, dev):
        return pltpu.make_async_remote_copy(
            src_ref=src, dst_ref=dst, send_sem=snd, recv_sem=sem, device_id=dev, device_id_type=MESH
        )

    def send(src, dst, sem, dev):
        remote(src, dst, sem, dev).start()
        pending.append((1, src))

    def send_all(count, start, sample):
        def step(d, _):
            start(d)
            return 0

        lax.fori_loop(1, count + 1, step, 0)
        pending.append((count, sample))

    def landed(ref, sem):
        pltpu.make_async_copy(ref, ref, sem).wait()

    def drain():
        for count, ref in pending:

            def step(_, carry):
                landed(ref, snd)
                return carry

            lax.fori_loop(0, count, step, 0)
        pending.clear()

    barrier = pltpu.get_barrier_semaphore()

    def greet_seq(d, _):
        pl.semaphore_signal(barrier, inc=1, device_id=seq_peer(lax.rem(s + d, 16)), device_id_type=MESH)
        return 0

    def greet_dp(d, _):
        pl.semaphore_signal(barrier, inc=1, device_id=dp_peer(lax.rem(dp + d, 8)), device_id_type=MESH)
        return 0

    lax.fori_loop(1, 16, greet_seq, 0)
    lax.fori_loop(1, 8, greet_dp, 0)
    loads = [
        pltpu.make_async_copy(src, dst, load_sem.at[n])
        for n, (src, dst) in enumerate(((cot_hbm, cot), (up_hbm, up), (res_hbm, res)))
    ]
    loads[0].start()
    loads[1].start()
    pl.semaphore_wait(barrier, 22)

    def send_head(h):
        def columns(p):
            return pl.ds(pl.multiple_of(p * 256 + h * HEAD, HEAD), HEAD)

        def start(d):
            p = lax.rem(s + d, 16)
            for a, src in enumerate((q, k, v)):
                remote(src.at[:, columns(p)], qkv.at[h, a, own], qkv_sem.at[h], seq_peer(p)).start()

        for a, src in enumerate((q, k, v)):
            pltpu.make_async_copy(src.at[:, columns(s)], qkv.at[h, a, own], qkv_sem.at[h]).start()
        send_all(15, start, qkv.at[0, 0, pl.ds(0, 3 * TOK)])

    send_head(0)
    loads[2].start()

    bias[...] = jnp.where(lax.broadcasted_iota(jnp.int32, (SEQLEN, HEAD), 0) < len_ref[0], 0.0, -1e30)
    loads[0].wait()
    loads[1].wait()

    def scaled(cols):
        return (cot[:, cols].astype(F32) * gate[:, cols]).astype(BF16)

    low_grad = jnp.zeros((TOK, RANK), F32)
    for t in range(5):
        cols = slice(t * 1024, (t + 1) * 1024)
        low_grad += lax.dot_general(scaled(cols), up[:, cols], (((1,), (1,)), ((), ())), preferred_element_type=F32)
    half_own = pl.ds(pl.multiple_of(c * TOK, TOK), TOK)
    lgc[half_own, :] = jnp.zeros((TOK, HEAD), BF16)
    lgc[half_own, 0:RANK] = low_grad.astype(BF16)
    send(lgc.at[half_own], lgc.at[half_own], lg_sem, other)

    for h in range(2):
        for t in range(8):
            dn[h, :, t * HEAD : (t + 1) * HEAD] = down[:, pl.ds(pl.multiple_of(512 * t + 256 * c + 128 * h, HEAD), HEAD)]

    drain()
    send_head(1)

    def attend(h, between):
        def chunk(i, carry):
            zz = lax.rem(z + 1 + i, 4)
            rows = pl.ds(pl.multiple_of(zz * BQ, BQ), BQ)
            queries = qkv[h, 0, rows, :]
            scores, top = [], None
            for t in range(SEQLEN // KC):
                keys = slice(t * KC, (t + 1) * KC)
                part = lax.dot_general(qkv[h, 1, keys, :], queries, (((1,), (1,)), ((), ())), preferred_element_type=F32)
                part = part + jnp.concatenate([bias[keys, :]] * (BQ // HEAD), 1)
                scores.append(part)
                largest = jnp.max(part, axis=0, keepdims=True)
                top = largest if top is None else jnp.maximum(top, largest)
            top = top * SCALE
            mixed, weight = None, None
            for t in range(SEQLEN // KC):
                keys = slice(t * KC, (t + 1) * KC)
                powers = jnp.exp2(scores[t] * SCALE - top)
                summed = jnp.sum(powers, axis=0, keepdims=True)
                product = lax.dot_general(
                    qkv[h, 2, keys, :], powers.astype(BF16), (((0,), (0,)), ((), ())), preferred_element_type=F32
                )
                mixed = product if mixed is None else mixed + product
                weight = summed if weight is None else weight + summed
            mixed = mixed / weight
            att[h, rows, :] = mixed.T.astype(BF16)

            def piece(yy):
                src = att.at[h, pl.ds(pl.multiple_of(zz * BQ + yy * CHIP, CHIP), CHIP), :]
                return src, ag.at[h, x, :, pl.ds(pl.multiple_of(j * HEAD, HEAD), HEAD)]

            src, dst = piece(1 - yh)
            remote(src, dst, ag_sem.at[h], chip_peer(zz * 2 + 1 - yh)).start()
            src, dst = piece(yh)

            @pl.when(i < 3)
            def _():
                remote(src, dst, ag_sem.at[h], chip_peer(zz * 2 + yh)).start()

            @pl.when(i == 3)
            def _():
                pltpu.make_async_copy(src, dst, ag_sem.at[h]).start()

            for when, action in between.items():
                pl.when(i == when)(action)
            return carry

        lax.fori_loop(0, SEQLEN // BQ, chunk, 0)
        pending.append((7, att.at[0, pl.ds(0, CHIP), :]))

    def piece_columns(n):
        return pl.ds(pl.multiple_of(n * 256, 256), 256)

    def send_weights(n, sem):
        for h in range(2):
            cols = pl.ds(pl.multiple_of(x * QUARTER + n * 256, 256), 256)
            src = w.at[pl.ds(h * HEAD, HEAD), cols]
            dst = wq.at[h, pl.ds(pl.multiple_of(j * HEAD, HEAD), HEAD), piece_columns(n)]
            pltpu.make_async_copy(src, dst, sem).start()
            send_all(
                7,
                lambda d, src=src, dst=dst: remote(src, dst, sem, chip_peer(lax.rem(j + d, 8))).start(),
                wq.at[0, pl.ds(0, HEAD), pl.ds(0, 256)],
            )

    def swap_weights():
        shared = wq.at[:, :, piece_columns(yl)]
        landed(shared, wq_sem.at[0])
        remote(shared, shared, wl_sem, {"yl": 1 - yl}).start()

    def forward(h):
        landed(ag.at[h, x], ag_sem.at[h])
        remote(ag.at[h, x], ag.at[h, x], f1_sem.at[h, 0], {"x": right}).start()
        remote(ag.at[h, x], ag.at[h, x], f1_sem.at[h, 1], {"x": left}).start()

    def forward_on(h):
        for n, (source, target) in enumerate(((left, right), (right, left))):
            landed(ag.at[h, source], f1_sem.at[h, n])
            half = ag.at[h, source, pl.ds(n * TOK, TOK)]
            send(half, half, f2_sem.at[h], {"x": target})

    landed(qkv.at[0], qkv_sem.at[0])
    attend(0, {})
    landed(qkv.at[1], qkv_sem.at[1])
    send_weights(yl, wq_sem.at[0])
    attend(1, {1: lambda: forward(0), 2: swap_weights})
    pending.append((2, ag.at[0, 0]))
    pending.append((1, wq.at[:, :, pl.ds(0, 256)]))
    send_weights(2, wq_sem.at[1])
    send_weights(3, wq_sem.at[2])

    forward_on(0)
    forward(1)
    pending.append((2, ag.at[0, 0]))

    l0[...] = jnp.zeros((CHIP, HEAD), F32)
    l0[:, 0:RANK] = lax.dot_general(
        ag[0, x], dn[0], (((1,), (1,)), ((), ())), preferred_element_type=F32
    ) + lax.dot_general(ag[1, x], dn[1], (((1,), (1,)), ((), ())), preferred_element_type=F32)
    send(l0.at[pl.ds((1 - c) * TOK, TOK)], l1, lr_sem, other)
    landed(l1, lr_sem)
    low[...] = (l0[pl.ds(c * TOK, TOK), 0:RANK] + l1[:, 0:RANK]).astype(BF16)

    for t in range(5):
        cols = slice(t * 1024, (t + 1) * 1024)
        gup[:, cols] = lax.dot_general(low[...], scaled(cols), (((0,), (0,)), ((), ())), preferred_element_type=F32).astype(BF16)
    send(gup.at[pl.ds((1 - c) * 32, 32)], g0, g0_sem, other)
    landed(g0, g0_sem)
    gs[...] = (gup[pl.ds(c * 32, 32), :].astype(F32) + g0[...].astype(F32)).astype(BF16)

    landed(lgc.at[pl.ds(0, TOK)], lg_sem)
    for h in range(2):
        gdq[h] = lax.dot_general(lgc[...], ag[h, x], (((0,), (0,)), ((), ())), preferred_element_type=F32)[0:RANK].astype(BF16)

    def columns640(p):
        return pl.ds(pl.multiple_of(p * 640, 640), 640)

    pltpu.make_async_copy(gs.at[:, columns640(j)], g1.at[j], g1_sem).start()
    send_all(
        7,
        lambda d: remote(gs.at[:, columns640(lax.rem(j + d, 8))], g1.at[j], g1_sem, chip_peer(lax.rem(j + d, 8))).start(),
        g1.at[0],
    )

    def head_columns(p):
        return pl.ds(pl.multiple_of(p * HEAD, HEAD), HEAD)

    pltpu.make_async_copy(gdq.at[:, :, head_columns(j)], g1d.at[j], g1d_sem).start()
    send_all(
        7,
        lambda d: remote(gdq.at[:, :, head_columns(lax.rem(j + d, 8))], g1d.at[j], g1d_sem, chip_peer(lax.rem(j + d, 8))).start(),
        g1d.at[0],
    )
    send_weights(4, wq_sem.at[3])
    forward_on(1)

    def total_of(ref):
        total = ref[0].astype(F32)
        for t in range(1, 8):
            total = total + ref[t].astype(F32)
        return total

    landed(g1, g1_sem)
    g2u[dp] = total_of(g1).astype(BF16)
    landed(g1d, g1d_sem)
    total = total_of(g1d)
    for h in range(2):
        g2d[dp, :, h * HEAD : (h + 1) * HEAD] = total[h].astype(BF16)
    send_all(
        7,
        lambda d: remote(g2d.at[dp], g2d.at[dp], g2d_sem, dp_peer(lax.rem(dp + d, 8))).start(),
        g2d.at[0],
    )
    send_all(
        7,
        lambda d: remote(g2u.at[dp], g2u.at[dp], g2u_sem, dp_peer(lax.rem(dp + d, 8))).start(),
        g2u.at[0],
    )

    groups = ((0, 3), (3, 2))

    def group_columns(g):
        first, count = groups[g]
        return pl.ds(first * 256, count * 256)

    def project(g, n, xx):
        def block(t, _):
            cols = piece_columns(t)
            part = jnp.dot(ag[0, xx], wq[0, :, cols], preferred_element_type=F32)
            part += jnp.dot(ag[1, xx], wq[1, :, cols], preferred_element_type=F32)
            first, second = part[:TOK], part[TOK:]
            pk[n, :, cols] = jnp.where(c == 0, first, second).astype(BF16)
            ps[n, :, cols] = jnp.where(c == 0, second, first).astype(BF16)
            return 0

        lax.fori_loop(groups[g][0], sum(groups[g]), block, 0)
        cols = group_columns(g)
        send(ps.at[n, :, cols], pr.at[n, :, cols], pr_sem.at[g, n], other)

    def finish(g, n, xx):
        cols = group_columns(g)
        landed(pr.at[n, :, cols], pr_sem.at[g, n])
        pk[n, :, cols] = (pk[n, :, cols].astype(F32) + pr[n, :, cols].astype(F32)).astype(BF16)
        if n:
            send(pk.at[n, :, cols], yb.at[x, :, cols], yb_sem.at[g, x], {"x": xx})

    far = lax.rem(x + 2, 4)

    def run_group(g):
        project(g, 1, right)
        project(g, 2, left)
        finish(g, 1, right)
        if g == 0:
            for h in range(2):
                landed(ag.at[h, far], f2_sem.at[h])
        project(g, 3, far)
        finish(g, 2, left)
        project(g, 0, x)
        finish(g, 3, far)
        finish(g, 0, x)

    landed(wq.at[:, :, pl.ds(0, 256)], wl_sem)
    landed(wq.at[:, :, pl.ds(0, 256)], wq_sem.at[1])
    run_group(0)

    landed(g2d.at[pl.ds(0, 7)], g2d_sem)
    gda[c, j] = total_of(g2d).astype(BF16)
    landed(g2u.at[pl.ds(0, 7)], g2u_sem)
    g3u[j] = total_of(g2u).astype(BF16)
    send_all(
        7,
        lambda d: remote(g3u.at[j], g3u.at[j], g3u_sem, chip_peer(lax.rem(j + d, 8))).start(),
        g3u.at[0],
    )
    send_all(
        7,
        lambda d: remote(gda.at[c, j], gda.at[c, j], g3d_sem, chip_peer(lax.rem(j + d, 8))).start(),
        gda.at[0, 0],
    )

    landed(wq.at[:, :, pl.ds(0, 256)], wq_sem.at[2])
    landed(wq.at[:, :, pl.ds(0, 256)], wq_sem.at[3])
    run_group(1)
    loads[2].wait()

    def write(g, base, xx):
        first, count = groups[g]
        cols = pl.ds(pl.multiple_of(xx * QUARTER + first * 256, 256), count * 256)
        delta = jnp.dot(low[...], up[:, cols], preferred_element_type=F32)
        out[:, cols] = (res[:, cols].astype(F32) + gate[:, cols] * (base.astype(F32) + delta)).astype(BF16)

    for g in range(2):
        write(g, pk[0, :, group_columns(g)], x)
    landed(g3u.at[pl.ds(0, 7)], g3u_sem)
    landed(gda.at[0, pl.ds(0, 7)], g3d_sem)
    send(g3u, g1, g4_sem.at[0], other)
    send(gda.at[c], gda.at[c], g4_sem.at[1], other)
    for g in range(2):
        for xx in (right, left, far):
            landed(yb.at[xx, :, group_columns(g)], yb_sem.at[g, xx])
            write(g, yb[xx, :, group_columns(g)], xx)
    landed(g1, g4_sem.at[0])
    landed(gda.at[0], g4_sem.at[1])
    rows_own, rows_other = (pl.ds(pl.multiple_of(r * 32, 32), 32) for r in (c, 1 - c))
    for t in range(8):
        gu[rows_own, t * 640 : (t + 1) * 640] = g3u[t].astype(F32)
        gu[rows_other, t * 640 : (t + 1) * 640] = g1[t].astype(F32)
        for cc in range(2):
            gd[:, (2 * t + cc) * 256 : (2 * t + cc + 1) * 256] = gda[cc, t].astype(F32)
    drain()


def on_device(q, k, v, res, gate, w, down, up, cot, lengths):
    vmem = pl.BlockSpec(memory_space=pltpu.VMEM)
    hbm = pl.BlockSpec(memory_space=pl.ANY)
    dma = pltpu.SemaphoreType.DMA
    out, gd, gu = pl.pallas_call(
        kernel,
        out_shape=(
            jax.ShapeDtypeStruct((TOK, D), BF16),
            jax.ShapeDtypeStruct((RANK, 4096), F32),
            jax.ShapeDtypeStruct((RANK, D), F32),
        ),
        in_specs=[pl.BlockSpec(memory_space=pltpu.SMEM), hbm, hbm, hbm, hbm, vmem, hbm, vmem, hbm, hbm],
        out_specs=(vmem, vmem, vmem),
        scratch_shapes=[
            pltpu.VMEM((2, 3, SEQLEN, HEAD), BF16),
            pltpu.VMEM((SEQLEN, HEAD), F32),
            pltpu.VMEM((2, SEQLEN, HEAD), BF16),
            pltpu.VMEM((2, 4, CHIP, 1024), BF16),
            pltpu.VMEM((2, 1024, QUARTER), BF16),
            pltpu.VMEM((CHIP, HEAD), BF16),
            pltpu.VMEM((2, RANK, 1024), BF16),
            pltpu.VMEM((TOK, RANK), BF16),
            pltpu.VMEM((4, TOK, QUARTER), BF16),
            pltpu.VMEM((4, TOK, QUARTER), BF16),
            pltpu.VMEM((4, TOK, QUARTER), BF16),
            pltpu.VMEM((4, TOK, QUARTER), BF16),
            pltpu.VMEM((TOK, D), BF16),
            pltpu.VMEM((RANK, D), BF16),
            pltpu.VMEM((TOK, D), BF16),
            pltpu.VMEM((RANK, D), BF16),
            pltpu.VMEM((CHIP, HEAD), F32),
            pltpu.VMEM((TOK, HEAD), F32),
            pltpu.VMEM((32, D), BF16),
            pltpu.VMEM((32, D), BF16),
            pltpu.VMEM((8, 32, 640), BF16),
            pltpu.VMEM((2, RANK, 1024), BF16),
            pltpu.VMEM((8, 2, RANK, HEAD), BF16),
            pltpu.VMEM((8, 32, 640), BF16),
            pltpu.VMEM((8, RANK, 256), BF16),
            pltpu.VMEM((8, 32, 640), BF16),
            pltpu.VMEM((2, 8, RANK, 256), BF16),
            dma,
            dma((3,)),
            dma((2,)),
            dma,
            dma((2,)),
            dma((4,)),
            dma,
            dma((2, 2)),
            dma((2,)),
            dma,
            dma,
            dma,
            dma,
            dma,
            dma,
            dma,
            dma,
            dma((2,)),
            dma((2, 4)),
            dma((2, 4)),
        ],
        compiler_params=pltpu.CompilerParams(collective_id=1, has_side_effects=True, vmem_limit_bytes=63 * 2**20),
        cost_estimate=pl.CostEstimate(flops=18 * 10**9, bytes_accessed=30 * 10**6, transcendentals=19 * 10**6),
    )(lengths, q[0], k[0], v[0], res[0], gate, w, down.T, up, cot[0])
    return out[None], gd.T, gu


def solution(mesh):
    inner = Mesh(mesh.devices.reshape(4, 2, 4, 2, 2), AXES)
    return jax.shard_map(
        on_device,
        mesh=inner,
        in_specs=(
            P(DP, SEQ, None),
            P(DP, SEQ, None),
            P(DP, SEQ, None),
            P(DP, SEQ, None),
            P(DP, None),
            P(SEQ, None),
            P(),
            P(),
            P(DP, SEQ, None),
            P(DP),
        ),
        out_specs=(P(DP, SEQ, None), P(), P()),
        check_vma=False,
    )
```

```python
import jax
import jax.numpy as jnp
import numpy as np
from jax import lax
from jax.experimental import pallas as pl
from jax.experimental.pallas import tpu as pltpu
from jax.sharding import Mesh
from jax.sharding import PartitionSpec as P

AXES = ("x", "yl", "z", "yh", "c")
DP = ("x", "yl")
SEQ = ("z", "yh", "c")
MESH = pl.DeviceIdType.MESH
HEAD = 128
RANK = 64
TOK = 192
CHIP = 2 * TOK
SEQLEN = 3072
D = 5120
QUARTER = D // 4
BQ = 768
KC = 512
SCALE = float(HEAD**-0.5 * np.log2(np.e))
F32 = jnp.float32
BF16 = jnp.bfloat16


def kernel(
    len_ref, q, k, v, res_hbm, gate, w, down, up_hbm, cot_hbm,
    out, gd, gu,
    qkv, bias, att, ag, wq, lgc, dn, low, ps, pk, pr, yb,
    res, up, cot, gup, l0, l1, g0, gs, g1, gdq, g1d, g2u, g2d, g3u, gda,
    snd, load_sem, qkv_sem, lg_sem, ag_sem, wq_sem, wl_sem, f1_sem, f2_sem, lr_sem, g0_sem, g1_sem, g1d_sem, g2u_sem, g2d_sem,
    g3u_sem, g3d_sem, g4_sem, pr_sem, yb_sem,
):
    x, yl, z, yh, c = (lax.axis_index(a) for a in AXES)
    s = z * 4 + yh * 2 + c
    j = z * 2 + yh
    dp = x * 2 + yl
    right, left = lax.rem(x + 1, 4), lax.rem(x + 3, 4)
    own = pl.ds(s * TOK, TOK)
    pending = []

    def seq_peer(p):
        return {"z": p // 4, "yh": lax.rem(p, 4) // 2, "c": lax.rem(p, 2)}

    def chip_peer(p):
        return {"z": p // 2, "yh": lax.rem(p, 2)}

    def dp_peer(p):
        return {"x": p // 2, "yl": lax.rem(p, 2)}

    other = {"c": 1 - c}

    def across(zz):
        return {"z": zz, "yh": 1 - yh, "yl": 1 - yl}


    def remote(src, dst, sem, dev):
        return pltpu.make_async_remote_copy(
            src_ref=src, dst_ref=dst, send_sem=snd, recv_sem=sem, device_id=dev, device_id_type=MESH
        )

    def send(src, dst, sem, dev):
        remote(src, dst, sem, dev).start()
        pending.append((1, src))

    def send_all(count, start, sample):
        def step(d, _):
            start(d)
            return 0

        lax.fori_loop(1, count + 1, step, 0)
        if sample is not None:
            pending.append((count, sample))

    def landed(ref, sem):
        pltpu.make_async_copy(ref, ref, sem).wait()

    def drain():
        for count, ref in pending:

            def step(_, carry):
                landed(ref, snd)
                return carry

            lax.fori_loop(0, count, step, 0)
        pending.clear()

    barrier = pltpu.get_barrier_semaphore()

    def greet_seq(d, _):
        pl.semaphore_signal(barrier, inc=1, device_id=seq_peer(lax.rem(s + d, 16)), device_id_type=MESH)
        return 0

    def greet_dp(d, _):
        pl.semaphore_signal(barrier, inc=1, device_id=dp_peer(lax.rem(dp + d, 8)), device_id_type=MESH)
        return 0

    lax.fori_loop(1, 16, greet_seq, 0)
    lax.fori_loop(1, 8, greet_dp, 0)
    for zz in range(4):
        pl.semaphore_signal(barrier, inc=1, device_id=across(zz), device_id_type=MESH)
    loads = [
        pltpu.make_async_copy(src, dst, load_sem.at[n])
        for n, (src, dst) in enumerate(((cot_hbm, cot), (up_hbm, up), (res_hbm, res)))
    ]
    loads[0].start()
    loads[1].start()
    pl.semaphore_wait(barrier, 26)

    def send_head(h):
        def columns(p):
            return pl.ds(pl.multiple_of(p * 256 + h * HEAD, HEAD), HEAD)

        def start(d):
            p = lax.rem(s + d, 16)
            for a, src in enumerate((q, k, v)):
                remote(src.at[:, columns(p)], qkv.at[h, a, own], qkv_sem.at[h], seq_peer(p)).start()

        for a, src in enumerate((q, k, v)):
            pltpu.make_async_copy(src.at[:, columns(s)], qkv.at[h, a, own], qkv_sem.at[h]).start()
        send_all(15, start, None)
        pending.append((1, qkv.at[0, :, pl.ds(0, 15 * TOK)]))

    send_head(0)
    loads[2].start()

    bias[...] = jnp.where(lax.broadcasted_iota(jnp.int32, (SEQLEN, HEAD), 0) < len_ref[0], 0.0, -1e30)
    loads[0].wait()
    loads[1].wait()

    def scaled(cols):
        return (cot[:, cols].astype(F32) * gate[:, cols]).astype(BF16)

    low_grad = jnp.zeros((TOK, RANK), F32)
    for t in range(5):
        cols = slice(t * 1024, (t + 1) * 1024)
        low_grad += lax.dot_general(scaled(cols), up[:, cols], (((1,), (1,)), ((), ())), preferred_element_type=F32)
    half_own = pl.ds(pl.multiple_of(c * TOK, TOK), TOK)
    lgc[half_own, :] = jnp.zeros((TOK, HEAD), BF16)
    lgc[half_own, 0:RANK] = low_grad.astype(BF16)
    send(lgc.at[half_own], lgc.at[half_own], lg_sem, other)

    for h in range(2):
        for t in range(8):
            dn[h, :, t * HEAD : (t + 1) * HEAD] = down[:, pl.ds(pl.multiple_of(512 * t + 256 * c + 128 * h, HEAD), HEAD)]

    drain()
    send_head(1)

    def attend(h, between):
        def chunk(i, carry):
            zz = lax.rem(z + 1 + i, 4)
            rows = pl.ds(pl.multiple_of(zz * BQ, BQ), BQ)
            queries = qkv[h, 0, rows, :]
            scores, top = [], None
            for t in range(SEQLEN // KC):
                keys = slice(t * KC, (t + 1) * KC)
                part = lax.dot_general(qkv[h, 1, keys, :], queries, (((1,), (1,)), ((), ())), preferred_element_type=F32)
                part = part + jnp.concatenate([bias[keys, :]] * (BQ // HEAD), 1)
                scores.append(part)
                largest = jnp.max(part, axis=0, keepdims=True)
                top = largest if top is None else jnp.maximum(top, largest)
            top = top * SCALE
            mixed, weight = None, None
            for t in range(SEQLEN // KC):
                keys = slice(t * KC, (t + 1) * KC)
                powers = jnp.exp2(scores[t] * SCALE - top)
                summed = jnp.sum(powers, axis=0, keepdims=True)
                product = lax.dot_general(
                    qkv[h, 2, keys, :], powers.astype(BF16), (((0,), (0,)), ((), ())), preferred_element_type=F32
                )
                mixed = product if mixed is None else mixed + product
                weight = summed if weight is None else weight + summed
            mixed = mixed / weight
            att[h, rows, :] = mixed.T.astype(BF16)

            def piece(yy):
                src = att.at[h, pl.ds(pl.multiple_of(zz * BQ + yy * CHIP, CHIP), CHIP), :]
                return src, ag.at[h, x, :, pl.ds(pl.multiple_of(j * HEAD, HEAD), HEAD)]

            src, dst = piece(1 - yh)
            remote(src, dst, ag_sem.at[h], chip_peer(zz * 2 + 1 - yh)).start()
            src, dst = piece(yh)

            @pl.when(i < 3)
            def _():
                remote(src, dst, ag_sem.at[h], chip_peer(zz * 2 + yh)).start()

            @pl.when(i == 3)
            def _():
                pltpu.make_async_copy(src, dst, ag_sem.at[h]).start()

            for when, action in between.items():
                pl.when(i == when)(action)
            return carry

        lax.fori_loop(0, SEQLEN // BQ, chunk, 0)
        pending.append((1, att.at[0, pl.ds(0, 7 * CHIP), :]))

    def piece_columns(n):
        return pl.ds(pl.multiple_of(n * 256, 256), 256)

    def send_weights(mine, theirs, sem):
        place = pl.ds(pl.multiple_of(j * HEAD, HEAD), HEAD)
        for h in range(2):

            def piece(n):
                cols = pl.ds(pl.multiple_of(x * QUARTER + n * 256, 256), 256)
                return w.at[pl.ds(h * HEAD, HEAD), cols], wq.at[h, place, piece_columns(n)]

            near, far = piece(mine), piece(theirs)
            pltpu.make_async_copy(*near, sem).start()

            def start(d, near=near, far=far):
                remote(*far, sem, across(lax.rem(z + d, 4))).start()

                @pl.when(d < 4)
                def _():
                    remote(*near, sem, {"z": lax.rem(z + d, 4)}).start()

            send_all(4, start, None)
            pending.append((1, wq.at[0, pl.ds(0, 7 * HEAD), pl.ds(0, 256)]))

    def swap_weights():
        shared = wq.at[:, :, piece_columns(yl)]
        landed(shared, wq_sem.at[0])
        remote(shared, shared, wl_sem, {"yl": 1 - yl}).start()

    def forward(h):
        landed(ag.at[h, x], ag_sem.at[h])
        remote(ag.at[h, x], ag.at[h, x], f1_sem.at[h, 0], {"x": right}).start()
        remote(ag.at[h, x], ag.at[h, x], f1_sem.at[h, 1], {"x": left}).start()

    def forward_on(h):
        for n, (source, target) in enumerate(((left, right), (right, left))):
            landed(ag.at[h, source], f1_sem.at[h, n])
            half = ag.at[h, source, pl.ds(n * TOK, TOK)]
            send(half, half, f2_sem.at[h], {"x": target})

    landed(qkv.at[0], qkv_sem.at[0])
    attend(0, {})
    landed(qkv.at[1], qkv_sem.at[1])
    send_weights(yl, 1 - yl, wq_sem.at[0])
    attend(1, {2: lambda: forward(0)})
    pending.append((2, ag.at[0, 0]))
    pending.append((1, wq.at[:, :, pl.ds(0, 256)]))
    send_weights(2, 2, wq_sem.at[1])
    swap_weights()

    forward_on(0)
    forward(1)
    pending.append((2, ag.at[0, 0]))

    l0[...] = jnp.zeros((CHIP, HEAD), F32)
    l0[:, 0:RANK] = lax.dot_general(
        ag[0, x], dn[0], (((1,), (1,)), ((), ())), preferred_element_type=F32
    ) + lax.dot_general(ag[1, x], dn[1], (((1,), (1,)), ((), ())), preferred_element_type=F32)
    send(l0.at[pl.ds((1 - c) * TOK, TOK)], l1, lr_sem, other)
    landed(l1, lr_sem)
    low[...] = (l0[pl.ds(c * TOK, TOK), 0:RANK] + l1[:, 0:RANK]).astype(BF16)

    for t in range(5):
        cols = slice(t * 1024, (t + 1) * 1024)
        gup[:, cols] = lax.dot_general(low[...], scaled(cols), (((0,), (0,)), ((), ())), preferred_element_type=F32).astype(BF16)
    send(gup.at[pl.ds((1 - c) * 32, 32)], g0, g0_sem, other)
    landed(lgc.at[pl.ds(0, TOK)], lg_sem)
    for h in range(2):
        gdq[h] = lax.dot_general(lgc[...], ag[h, x], (((0,), (0,)), ((), ())), preferred_element_type=F32)[0:RANK].astype(BF16)

    landed(g0, g0_sem)
    gs[...] = (gup[pl.ds(c * 32, 32), :].astype(F32) + g0[...].astype(F32)).astype(BF16)

    def columns640(p):
        return pl.ds(pl.multiple_of(p * 640, 640), 640)

    pltpu.make_async_copy(gs.at[:, columns640(j)], g1.at[j], g1_sem).start()
    send_all(
        7,
        lambda d: remote(gs.at[:, columns640(lax.rem(j + d, 8))], g1.at[j], g1_sem, chip_peer(lax.rem(j + d, 8))).start(),
        g1.at[0],
    )

    def head_columns(p):
        return pl.ds(pl.multiple_of(p * HEAD, HEAD), HEAD)

    pltpu.make_async_copy(gdq.at[:, :, head_columns(j)], g1d.at[j], g1d_sem).start()
    send_all(
        7,
        lambda d: remote(gdq.at[:, :, head_columns(lax.rem(j + d, 8))], g1d.at[j], g1d_sem, chip_peer(lax.rem(j + d, 8))).start(),
        g1d.at[0],
    )
    send_weights(3, 3, wq_sem.at[2])
    send_weights(4, 4, wq_sem.at[3])
    forward_on(1)

    def total_of(ref):
        total = ref[0].astype(F32)
        for t in range(1, 8):
            total = total + ref[t].astype(F32)
        return total

    landed(g1, g1_sem)
    g2u[dp] = total_of(g1).astype(BF16)
    landed(g1d, g1d_sem)
    total = total_of(g1d)
    for h in range(2):
        g2d[dp, :, h * HEAD : (h + 1) * HEAD] = total[h].astype(BF16)
    send_all(
        7,
        lambda d: remote(g2d.at[dp], g2d.at[dp], g2d_sem, dp_peer(lax.rem(dp + d, 8))).start(),
        g2d.at[0],
    )
    send_all(
        7,
        lambda d: remote(g2u.at[dp], g2u.at[dp], g2u_sem, dp_peer(lax.rem(dp + d, 8))).start(),
        g2u.at[0],
    )

    groups = ((0, 3), (3, 2))

    def group_columns(g):
        first, count = groups[g]
        return pl.ds(first * 256, count * 256)

    def project(g, n, xx):
        def block(t, _):
            cols = piece_columns(t)
            part = jnp.dot(ag[0, xx], wq[0, :, cols], preferred_element_type=F32)
            part += jnp.dot(ag[1, xx], wq[1, :, cols], preferred_element_type=F32)
            first, second = part[:TOK], part[TOK:]
            pk[n, :, cols] = jnp.where(c == 0, first, second).astype(BF16)
            ps[n, :, cols] = jnp.where(c == 0, second, first).astype(BF16)
            return 0

        lax.fori_loop(groups[g][0], sum(groups[g]), block, 0)
        cols = group_columns(g)
        send(ps.at[n, :, cols], pr.at[n, :, cols], pr_sem.at[g, n], other)

    def finish(g, n, xx):
        cols = group_columns(g)
        landed(pr.at[n, :, cols], pr_sem.at[g, n])
        pk[n, :, cols] = (pk[n, :, cols].astype(F32) + pr[n, :, cols].astype(F32)).astype(BF16)
        if n:
            send(pk.at[n, :, cols], yb.at[x, :, cols], yb_sem.at[g, x], {"x": xx})

    far = lax.rem(x + 2, 4)

    def run_group(g):
        project(g, 1, right)
        project(g, 2, left)
        finish(g, 1, right)
        if g == 0:
            for h in range(2):
                landed(ag.at[h, far], f2_sem.at[h])
        project(g, 3, far)
        finish(g, 2, left)
        project(g, 0, x)
        finish(g, 3, far)
        finish(g, 0, x)

    landed(wq.at[:, :, pl.ds(0, 256)], wl_sem)
    landed(wq.at[:, :, pl.ds(0, 256)], wq_sem.at[1])
    run_group(0)

    landed(g2d.at[pl.ds(0, 7)], g2d_sem)
    gda[c, j] = total_of(g2d).astype(BF16)
    landed(g2u.at[pl.ds(0, 7)], g2u_sem)
    g3u[j] = total_of(g2u).astype(BF16)
    send_all(
        7,
        lambda d: remote(g3u.at[j], g3u.at[j], g3u_sem, chip_peer(lax.rem(j + d, 8))).start(),
        g3u.at[0],
    )
    send_all(
        7,
        lambda d: remote(gda.at[c, j], gda.at[c, j], g3d_sem, chip_peer(lax.rem(j + d, 8))).start(),
        gda.at[0, 0],
    )

    landed(wq.at[:, :, pl.ds(0, 256)], wq_sem.at[2])
    landed(wq.at[:, :, pl.ds(0, 256)], wq_sem.at[3])
    run_group(1)
    loads[2].wait()

    def write(g, base, xx):
        first, count = groups[g]
        cols = pl.ds(pl.multiple_of(xx * QUARTER + first * 256, 256), count * 256)
        delta = jnp.dot(low[...], up[:, cols], preferred_element_type=F32)
        out[:, cols] = (res[:, cols].astype(F32) + gate[:, cols] * (base.astype(F32) + delta)).astype(BF16)

    for g in range(2):
        write(g, pk[0, :, group_columns(g)], x)
    landed(g3u.at[pl.ds(0, 7)], g3u_sem)
    landed(gda.at[0, pl.ds(0, 7)], g3d_sem)
    send(g3u, g1, g4_sem.at[0], other)
    send(gda.at[c], gda.at[c], g4_sem.at[1], other)
    for g in range(2):
        for xx in (right, left, far):
            landed(yb.at[xx, :, group_columns(g)], yb_sem.at[g, xx])
            write(g, yb[xx, :, group_columns(g)], xx)
    landed(g1, g4_sem.at[0])
    landed(gda.at[0], g4_sem.at[1])
    rows_own, rows_other = (pl.ds(pl.multiple_of(r * 32, 32), 32) for r in (c, 1 - c))
    for t in range(8):
        gu[rows_own, t * 640 : (t + 1) * 640] = g3u[t].astype(F32)
        gu[rows_other, t * 640 : (t + 1) * 640] = g1[t].astype(F32)
        for cc in range(2):
            gd[:, (2 * t + cc) * 256 : (2 * t + cc + 1) * 256] = gda[cc, t].astype(F32)
    drain()


def on_device(q, k, v, res, gate, w, down, up, cot, lengths):
    vmem = pl.BlockSpec(memory_space=pltpu.VMEM)
    hbm = pl.BlockSpec(memory_space=pl.ANY)
    dma = pltpu.SemaphoreType.DMA
    out, gd, gu = pl.pallas_call(
        kernel,
        out_shape=(
            jax.ShapeDtypeStruct((TOK, D), BF16),
            jax.ShapeDtypeStruct((RANK, 4096), F32),
            jax.ShapeDtypeStruct((RANK, D), F32),
        ),
        in_specs=[pl.BlockSpec(memory_space=pltpu.SMEM), hbm, hbm, hbm, hbm, vmem, hbm, vmem, hbm, hbm],
        out_specs=(vmem, vmem, vmem),
        scratch_shapes=[
            pltpu.VMEM((2, 3, SEQLEN, HEAD), BF16),
            pltpu.VMEM((SEQLEN, HEAD), F32),
            pltpu.VMEM((2, SEQLEN, HEAD), BF16),
            pltpu.VMEM((2, 4, CHIP, 1024), BF16),
            pltpu.VMEM((2, 1024, QUARTER), BF16),
            pltpu.VMEM((CHIP, HEAD), BF16),
            pltpu.VMEM((2, RANK, 1024), BF16),
            pltpu.VMEM((TOK, RANK), BF16),
            pltpu.VMEM((4, TOK, QUARTER), BF16),
            pltpu.VMEM((4, TOK, QUARTER), BF16),
            pltpu.VMEM((4, TOK, QUARTER), BF16),
            pltpu.VMEM((4, TOK, QUARTER), BF16),
            pltpu.VMEM((TOK, D), BF16),
            pltpu.VMEM((RANK, D), BF16),
            pltpu.VMEM((TOK, D), BF16),
            pltpu.VMEM((RANK, D), BF16),
            pltpu.VMEM((CHIP, HEAD), F32),
            pltpu.VMEM((TOK, HEAD), F32),
            pltpu.VMEM((32, D), BF16),
            pltpu.VMEM((32, D), BF16),
            pltpu.VMEM((8, 32, 640), BF16),
            pltpu.VMEM((2, RANK, 1024), BF16),
            pltpu.VMEM((8, 2, RANK, HEAD), BF16),
            pltpu.VMEM((8, 32, 640), BF16),
            pltpu.VMEM((8, RANK, 256), BF16),
            pltpu.VMEM((8, 32, 640), BF16),
            pltpu.VMEM((2, 8, RANK, 256), BF16),
            dma,
            dma((3,)),
            dma((2,)),
            dma,
            dma((2,)),
            dma((4,)),
            dma,
            dma((2, 2)),
            dma((2,)),
            dma,
            dma,
            dma,
            dma,
            dma,
            dma,
            dma,
            dma,
            dma((2,)),
            dma((2, 4)),
            dma((2, 4)),
        ],
        compiler_params=pltpu.CompilerParams(collective_id=1, has_side_effects=True, vmem_limit_bytes=63 * 2**20),
        cost_estimate=pl.CostEstimate(flops=18 * 10**9, bytes_accessed=30 * 10**6, transcendentals=19 * 10**6),
    )(lengths, q[0], k[0], v[0], res[0], gate, w, down.T, up, cot[0])
    return out[None], gd.T, gu


def solution(mesh):
    inner = Mesh(mesh.devices.reshape(4, 2, 4, 2, 2), AXES)
    return jax.shard_map(
        on_device,
        mesh=inner,
        in_specs=(
            P(DP, SEQ, None),
            P(DP, SEQ, None),
            P(DP, SEQ, None),
            P(DP, SEQ, None),
            P(DP, None),
            P(SEQ, None),
            P(),
            P(),
            P(DP, SEQ, None),
            P(DP),
        ),
        out_specs=(P(DP, SEQ, None), P(), P()),
        check_vma=False,
    )
```

```python
import jax
import jax.numpy as jnp
import numpy as np
from jax import lax
from jax.experimental import pallas as pl
from jax.experimental.pallas import tpu as pltpu
from jax.sharding import Mesh
from jax.sharding import PartitionSpec as P

AXES = ("x", "yl", "z", "yh", "c")
DP = ("x", "yl")
SEQ = ("z", "yh", "c")
MESH = pl.DeviceIdType.MESH
HEAD = 128
RANK = 64
TOK = 192
CHIP = 2 * TOK
SEQLEN = 3072
D = 5120
QUARTER = D // 4
BQ = 768
KC = 512
SCALE = float(HEAD**-0.5 * np.log2(np.e))
F32 = jnp.float32
BF16 = jnp.bfloat16


def kernel(
    len_ref, q, k, v, res_hbm, gate, w, down, up_hbm, cot_hbm,
    out, gd, gu,
    qkv, bias, att, ag, wq, lgc, dn, low, ps, pk, pr, yb,
    res, up, cot, gup, l0, l1, g0, gs, g1, gdq, g1d, g2u, g2d, g3u, gda,
    snd, load_sem, qkv_sem, lg_sem, ag_sem, wq_sem, wl_sem, f1_sem, f2_sem, lr_sem, g0_sem, g1_sem, g1d_sem, g2u_sem, g2d_sem,
    g3u_sem, g3d_sem, g4_sem, pr_sem, yb_sem,
):
    x, yl, z, yh, c = (lax.axis_index(a) for a in AXES)
    s = z * 4 + yh * 2 + c
    j = z * 2 + yh
    dp = x * 2 + yl
    right, left = lax.rem(x + 1, 4), lax.rem(x + 3, 4)
    own = pl.ds(s * TOK, TOK)
    pending = []

    def seq_peer(p):
        return {"z": p // 4, "yh": lax.rem(p, 4) // 2, "c": lax.rem(p, 2)}

    def chip_peer(p):
        return {"z": p // 2, "yh": lax.rem(p, 2)}

    def dp_peer(p):
        return {"x": p // 2, "yl": lax.rem(p, 2)}

    other = {"c": 1 - c}

    def across(zz):
        return {"z": zz, "yh": 1 - yh, "yl": 1 - yl}


    def remote(src, dst, sem, dev):
        return pltpu.make_async_remote_copy(
            src_ref=src, dst_ref=dst, send_sem=snd, recv_sem=sem, device_id=dev, device_id_type=MESH
        )

    def send(src, dst, sem, dev):
        remote(src, dst, sem, dev).start()
        pending.append((1, src))

    def send_all(count, start, sample):
        def step(d, _):
            start(d)
            return 0

        lax.fori_loop(1, count + 1, step, 0)
        if sample is not None:
            pending.append((count, sample))

    def landed(ref, sem):
        pltpu.make_async_copy(ref, ref, sem).wait()

    def drain():
        for count, ref in pending:

            def step(_, carry):
                landed(ref, snd)
                return carry

            lax.fori_loop(0, count, step, 0)
        pending.clear()

    barrier = pltpu.get_barrier_semaphore()

    def greet_seq(d, _):
        pl.semaphore_signal(barrier, inc=1, device_id=seq_peer(lax.rem(s + d, 16)), device_id_type=MESH)
        return 0

    def greet_dp(d, _):
        pl.semaphore_signal(barrier, inc=1, device_id=dp_peer(lax.rem(dp + d, 8)), device_id_type=MESH)
        return 0

    lax.fori_loop(1, 16, greet_seq, 0)
    lax.fori_loop(1, 8, greet_dp, 0)
    for zz in range(4):
        pl.semaphore_signal(barrier, inc=1, device_id=across(zz), device_id_type=MESH)
    loads = [
        pltpu.make_async_copy(src, dst, load_sem.at[n])
        for n, (src, dst) in enumerate(((cot_hbm, cot), (up_hbm, up), (res_hbm, res)))
    ]
    loads[0].start()
    loads[1].start()
    pl.semaphore_wait(barrier, 26)

    def send_head(h, which=(0, 1, 2)):
        def columns(p):
            return pl.ds(pl.multiple_of(p * 256 + h * HEAD, HEAD), HEAD)

        def start(d):
            p = lax.rem(s + d, 16)
            for a, src in ((a, (q, k, v)[a]) for a in which):
                remote(src.at[:, columns(p)], qkv.at[h, a, own], qkv_sem.at[h], seq_peer(p)).start()

        for a, src in ((a, (q, k, v)[a]) for a in which):
            pltpu.make_async_copy(src.at[:, columns(s)], qkv.at[h, a, own], qkv_sem.at[h]).start()
        send_all(15, start, None)
        pending.append((1, qkv.at[0, pl.ds(0, len(which)), pl.ds(0, 15 * TOK)]))

    send_head(0)
    loads[2].start()

    bias[...] = jnp.where(lax.broadcasted_iota(jnp.int32, (SEQLEN, HEAD), 0) < len_ref[0], 0.0, -1e30)
    loads[0].wait()
    loads[1].wait()

    def scaled(cols):
        return (cot[:, cols].astype(F32) * gate[:, cols]).astype(BF16)

    low_grad = jnp.zeros((TOK, RANK), F32)
    for t in range(5):
        cols = slice(t * 1024, (t + 1) * 1024)
        low_grad += lax.dot_general(scaled(cols), up[:, cols], (((1,), (1,)), ((), ())), preferred_element_type=F32)
    half_own = pl.ds(pl.multiple_of(c * TOK, TOK), TOK)
    lgc[half_own, :] = jnp.zeros((TOK, HEAD), BF16)
    lgc[half_own, 0:RANK] = low_grad.astype(BF16)
    send(lgc.at[half_own], lgc.at[half_own], lg_sem, other)

    for h in range(2):
        for t in range(8):
            dn[h, :, t * HEAD : (t + 1) * HEAD] = down[:, pl.ds(pl.multiple_of(512 * t + 256 * c + 128 * h, HEAD), HEAD)]

    drain()
    send_head(1, (0, 1))

    def attend(h, between):
        def chunk(i, carry):
            zz = lax.rem(z + 1 + i, 4)
            rows = pl.ds(pl.multiple_of(zz * BQ, BQ), BQ)
            queries = qkv[h, 0, rows, :]
            scores, top = [], None
            for t in range(SEQLEN // KC):
                keys = slice(t * KC, (t + 1) * KC)
                part = lax.dot_general(qkv[h, 1, keys, :], queries, (((1,), (1,)), ((), ())), preferred_element_type=F32)
                part = part + jnp.concatenate([bias[keys, :]] * (BQ // HEAD), 1)
                scores.append(part)
                largest = jnp.max(part, axis=0, keepdims=True)
                top = largest if top is None else jnp.maximum(top, largest)
            top = top * SCALE
            mixed, weight = None, None
            for t in range(SEQLEN // KC):
                keys = slice(t * KC, (t + 1) * KC)
                powers = jnp.exp2(scores[t] * SCALE - top)
                summed = jnp.sum(powers, axis=0, keepdims=True)
                product = lax.dot_general(
                    qkv[h, 2, keys, :], powers.astype(BF16), (((0,), (0,)), ((), ())), preferred_element_type=F32
                )
                mixed = product if mixed is None else mixed + product
                weight = summed if weight is None else weight + summed
            mixed = mixed / weight
            att[h, rows, :] = mixed.T.astype(BF16)

            def piece(yy):
                src = att.at[h, pl.ds(pl.multiple_of(zz * BQ + yy * CHIP, CHIP), CHIP), :]
                return src, ag.at[h, x, :, pl.ds(pl.multiple_of(j * HEAD, HEAD), HEAD)]

            src, dst = piece(1 - yh)
            remote(src, dst, ag_sem.at[h], chip_peer(zz * 2 + 1 - yh)).start()
            src, dst = piece(yh)

            @pl.when(i < 3)
            def _():
                remote(src, dst, ag_sem.at[h], chip_peer(zz * 2 + yh)).start()

            @pl.when(i == 3)
            def _():
                pltpu.make_async_copy(src, dst, ag_sem.at[h]).start()

            for when, action in between.items():
                pl.when(i == when)(action)
            return carry

        lax.fori_loop(0, SEQLEN // BQ, chunk, 0)
        pending.append((1, att.at[0, pl.ds(0, 7 * CHIP), :]))

    def piece_columns(n):
        return pl.ds(pl.multiple_of(n * 256, 256), 256)

    def send_weights(mine, theirs, sem):
        place = pl.ds(pl.multiple_of(j * HEAD, HEAD), HEAD)
        for h in range(2):

            def piece(n):
                cols = pl.ds(pl.multiple_of(x * QUARTER + n * 256, 256), 256)
                return w.at[pl.ds(h * HEAD, HEAD), cols], wq.at[h, place, piece_columns(n)]

            near, far = piece(mine), piece(theirs)
            pltpu.make_async_copy(*near, sem).start()

            def start(d, near=near, far=far):
                remote(*far, sem, across(lax.rem(z + d, 4))).start()

                @pl.when(d < 4)
                def _():
                    remote(*near, sem, {"z": lax.rem(z + d, 4)}).start()

            send_all(4, start, None)
            pending.append((1, wq.at[0, pl.ds(0, 7 * HEAD), pl.ds(0, 256)]))

    def swap_weights():
        shared = wq.at[:, :, piece_columns(yl)]
        landed(shared, wq_sem.at[0])
        remote(shared, shared, wl_sem, {"yl": 1 - yl}).start()

    def forward(h):
        landed(ag.at[h, x], ag_sem.at[h])
        remote(ag.at[h, x], ag.at[h, x], f1_sem.at[h, 0], {"x": right}).start()
        remote(ag.at[h, x], ag.at[h, x], f1_sem.at[h, 1], {"x": left}).start()

    def forward_on(h):
        for n, (source, target) in enumerate(((left, right), (right, left))):
            landed(ag.at[h, source], f1_sem.at[h, n])
            half = ag.at[h, source, pl.ds(n * TOK, TOK)]
            send(half, half, f2_sem.at[h], {"x": target})

    landed(qkv.at[0], qkv_sem.at[0])
    attend(0, {})
    send_head(1, (2,))
    forward(0)
    landed(qkv.at[1], qkv_sem.at[1])
    send_weights(yl, 1 - yl, wq_sem.at[0])
    attend(1, {})
    pending.append((2, ag.at[0, 0]))
    pending.append((1, wq.at[:, :, pl.ds(0, 256)]))
    send_weights(2, 2, wq_sem.at[1])
    swap_weights()

    forward_on(0)

    def grad_down_part(h):
        gdq[h] = lax.dot_general(lgc[...], ag[h, x], (((0,), (0,)), ((), ())), preferred_element_type=F32)[0:RANK].astype(BF16)

    def low_rank_part(h):
        return lax.dot_general(ag[h, x], dn[h], (((1,), (1,)), ((), ())), preferred_element_type=F32)

    landed(lgc.at[pl.ds(0, TOK)], lg_sem)
    grad_down_part(0)
    l0[...] = jnp.zeros((CHIP, HEAD), F32)
    l0[:, 0:RANK] = low_rank_part(0)
    forward(1)
    pending.append((2, ag.at[0, 0]))

    l0[:, 0:RANK] += low_rank_part(1)
    send(l0.at[pl.ds((1 - c) * TOK, TOK)], l1, lr_sem, other)
    grad_down_part(1)
    landed(l1, lr_sem)
    low[...] = (l0[pl.ds(c * TOK, TOK), 0:RANK] + l1[:, 0:RANK]).astype(BF16)

    for t in range(5):
        cols = slice(t * 1024, (t + 1) * 1024)
        gup[:, cols] = lax.dot_general(low[...], scaled(cols), (((0,), (0,)), ((), ())), preferred_element_type=F32).astype(BF16)
    send(gup.at[pl.ds((1 - c) * 32, 32)], g0, g0_sem, other)
    landed(g0, g0_sem)
    gs[...] = (gup[pl.ds(c * 32, 32), :].astype(F32) + g0[...].astype(F32)).astype(BF16)

    def columns640(p):
        return pl.ds(pl.multiple_of(p * 640, 640), 640)

    pltpu.make_async_copy(gs.at[:, columns640(j)], g1.at[j], g1_sem).start()
    send_all(
        7,
        lambda d: remote(gs.at[:, columns640(lax.rem(j + d, 8))], g1.at[j], g1_sem, chip_peer(lax.rem(j + d, 8))).start(),
        g1.at[0],
    )

    def head_columns(p):
        return pl.ds(pl.multiple_of(p * HEAD, HEAD), HEAD)

    pltpu.make_async_copy(gdq.at[:, :, head_columns(j)], g1d.at[j], g1d_sem).start()
    send_all(
        7,
        lambda d: remote(gdq.at[:, :, head_columns(lax.rem(j + d, 8))], g1d.at[j], g1d_sem, chip_peer(lax.rem(j + d, 8))).start(),
        g1d.at[0],
    )
    send_weights(3, 3, wq_sem.at[2])
    send_weights(4, 4, wq_sem.at[3])
    forward_on(1)

    def total_of(ref):
        total = ref[0].astype(F32)
        for t in range(1, 8):
            total = total + ref[t].astype(F32)
        return total

    def over_clips():
        landed(g1, g1_sem)
        g2u[dp] = total_of(g1).astype(BF16)
        landed(g1d, g1d_sem)
        total = total_of(g1d)
        for h in range(2):
            g2d[dp, :, h * HEAD : (h + 1) * HEAD] = total[h].astype(BF16)
        send_all(
            7,
            lambda d: remote(g2d.at[dp], g2d.at[dp], g2d_sem, dp_peer(lax.rem(dp + d, 8))).start(),
            g2d.at[0],
        )
        send_all(
            7,
            lambda d: remote(g2u.at[dp], g2u.at[dp], g2u_sem, dp_peer(lax.rem(dp + d, 8))).start(),
            g2u.at[0],
        )

    groups = ((0, 3), (3, 2))

    def group_columns(g):
        first, count = groups[g]
        return pl.ds(first * 256, count * 256)

    def project(g, n, xx):
        def block(t, _):
            cols = piece_columns(t)
            part = jnp.dot(ag[0, xx], wq[0, :, cols], preferred_element_type=F32)
            part += jnp.dot(ag[1, xx], wq[1, :, cols], preferred_element_type=F32)
            first, second = part[:TOK], part[TOK:]
            pk[n, :, cols] = jnp.where(c == 0, first, second).astype(BF16)
            ps[n, :, cols] = jnp.where(c == 0, second, first).astype(BF16)
            return 0

        lax.fori_loop(groups[g][0], sum(groups[g]), block, 0)
        cols = group_columns(g)
        send(ps.at[n, :, cols], pr.at[n, :, cols], pr_sem.at[g, n], other)

    def finish(g, n, xx):
        cols = group_columns(g)
        landed(pr.at[n, :, cols], pr_sem.at[g, n])
        pk[n, :, cols] = (pk[n, :, cols].astype(F32) + pr[n, :, cols].astype(F32)).astype(BF16)
        if n:
            send(pk.at[n, :, cols], yb.at[x, :, cols], yb_sem.at[g, x], {"x": xx})

    far = lax.rem(x + 2, 4)

    def run_group(g):
        project(g, 1, right)
        project(g, 2, left)
        if g == 0:
            over_clips()
        finish(g, 1, right)
        if g == 0:
            for h in range(2):
                landed(ag.at[h, far], f2_sem.at[h])
        project(g, 3, far)
        finish(g, 2, left)
        project(g, 0, x)
        finish(g, 3, far)
        finish(g, 0, x)

    landed(wq.at[:, :, pl.ds(0, 256)], wl_sem)
    landed(wq.at[:, :, pl.ds(0, 256)], wq_sem.at[1])
    run_group(0)

    landed(g2d.at[pl.ds(0, 7)], g2d_sem)
    gda[c, j] = total_of(g2d).astype(BF16)
    landed(g2u.at[pl.ds(0, 7)], g2u_sem)
    g3u[j] = total_of(g2u).astype(BF16)
    def spread(d):
        for ref, sem in ((g3u.at[j], g3u_sem), (gda.at[c, j], g3d_sem)):
            remote(ref, ref, sem, across(lax.rem(z + d, 4))).start()

            @pl.when(d < 4)
            def _():
                remote(ref, ref, sem, {"z": lax.rem(z + d, 4)}).start()

    send_all(4, spread, None)
    pending.append((1, g3u.at[pl.ds(0, 7)]))
    pending.append((1, gda.at[0, pl.ds(0, 7)]))

    landed(wq.at[:, :, pl.ds(0, 256)], wq_sem.at[2])
    landed(wq.at[:, :, pl.ds(0, 256)], wq_sem.at[3])
    run_group(1)
    loads[2].wait()

    def write(g, base, xx):
        first, count = groups[g]
        cols = pl.ds(pl.multiple_of(xx * QUARTER + first * 256, 256), count * 256)
        delta = jnp.dot(low[...], up[:, cols], preferred_element_type=F32)
        out[:, cols] = (res[:, cols].astype(F32) + gate[:, cols] * (base.astype(F32) + delta)).astype(BF16)

    for g in range(2):
        write(g, pk[0, :, group_columns(g)], x)
    landed(g3u.at[pl.ds(0, 7)], g3u_sem)
    landed(gda.at[0, pl.ds(0, 7)], g3d_sem)
    send(g3u, g1, g4_sem.at[0], other)
    send(gda.at[c], gda.at[c], g4_sem.at[1], other)
    for g in range(2):
        for xx in (right, left, far):
            landed(yb.at[xx, :, group_columns(g)], yb_sem.at[g, xx])
            write(g, yb[xx, :, group_columns(g)], xx)
    landed(g1, g4_sem.at[0])
    landed(gda.at[0], g4_sem.at[1])
    rows_own, rows_other = (pl.ds(pl.multiple_of(r * 32, 32), 32) for r in (c, 1 - c))
    for t in range(8):
        gu[rows_own, t * 640 : (t + 1) * 640] = g3u[t]
        gu[rows_other, t * 640 : (t + 1) * 640] = g1[t]
        for cc in range(2):
            gd[:, (2 * t + cc) * 256 : (2 * t + cc + 1) * 256] = gda[cc, t]
    drain()


def on_device(q, k, v, res, gate, w, down, up, cot, lengths):
    vmem = pl.BlockSpec(memory_space=pltpu.VMEM)
    hbm = pl.BlockSpec(memory_space=pl.ANY)
    dma = pltpu.SemaphoreType.DMA
    out, gd, gu = pl.pallas_call(
        kernel,
        out_shape=(
            jax.ShapeDtypeStruct((TOK, D), BF16),
            jax.ShapeDtypeStruct((RANK, 4096), BF16),
            jax.ShapeDtypeStruct((RANK, D), BF16),
        ),
        in_specs=[pl.BlockSpec(memory_space=pltpu.SMEM), hbm, hbm, hbm, hbm, vmem, hbm, vmem, hbm, hbm],
        out_specs=(vmem, vmem, vmem),
        scratch_shapes=[
            pltpu.VMEM((2, 3, SEQLEN, HEAD), BF16),
            pltpu.VMEM((SEQLEN, HEAD), F32),
            pltpu.VMEM((2, SEQLEN, HEAD), BF16),
            pltpu.VMEM((2, 4, CHIP, 1024), BF16),
            pltpu.VMEM((2, 1024, QUARTER), BF16),
            pltpu.VMEM((CHIP, HEAD), BF16),
            pltpu.VMEM((2, RANK, 1024), BF16),
            pltpu.VMEM((TOK, RANK), BF16),
            pltpu.VMEM((4, TOK, QUARTER), BF16),
            pltpu.VMEM((4, TOK, QUARTER), BF16),
            pltpu.VMEM((4, TOK, QUARTER), BF16),
            pltpu.VMEM((4, TOK, QUARTER), BF16),
            pltpu.VMEM((TOK, D), BF16),
            pltpu.VMEM((RANK, D), BF16),
            pltpu.VMEM((TOK, D), BF16),
            pltpu.VMEM((RANK, D), BF16),
            pltpu.VMEM((CHIP, HEAD), F32),
            pltpu.VMEM((TOK, HEAD), F32),
            pltpu.VMEM((32, D), BF16),
            pltpu.VMEM((32, D), BF16),
            pltpu.VMEM((8, 32, 640), BF16),
            pltpu.VMEM((2, RANK, 1024), BF16),
            pltpu.VMEM((8, 2, RANK, HEAD), BF16),
            pltpu.VMEM((8, 32, 640), BF16),
            pltpu.VMEM((8, RANK, 256), BF16),
            pltpu.VMEM((8, 32, 640), BF16),
            pltpu.VMEM((2, 8, RANK, 256), BF16),
            dma,
            dma((3,)),
            dma((2,)),
            dma,
            dma((2,)),
            dma((4,)),
            dma,
            dma((2, 2)),
            dma((2,)),
            dma,
            dma,
            dma,
            dma,
            dma,
            dma,
            dma,
            dma,
            dma((2,)),
            dma((2, 4)),
            dma((2, 4)),
        ],
        compiler_params=pltpu.CompilerParams(collective_id=1, has_side_effects=True, vmem_limit_bytes=63 * 2**20),
        cost_estimate=pl.CostEstimate(flops=18 * 10**9, bytes_accessed=30 * 10**6, transcendentals=19 * 10**6),
    )(lengths, q[0], k[0], v[0], res[0], gate, w, down.T, up, cot[0])
    return out[None], gd.T.astype(F32), gu.astype(F32)


def solution(mesh):
    inner = Mesh(mesh.devices.reshape(4, 2, 4, 2, 2), AXES)
    return jax.shard_map(
        on_device,
        mesh=inner,
        in_specs=(
            P(DP, SEQ, None),
            P(DP, SEQ, None),
            P(DP, SEQ, None),
            P(DP, SEQ, None),
            P(DP, None),
            P(SEQ, None),
            P(),
            P(),
            P(DP, SEQ, None),
            P(DP),
        ),
        out_specs=(P(DP, SEQ, None), P(), P()),
        check_vma=False,
    )
```
